512 devices in a mesh: rep: 4 (over z_hi), fsdp: 128 (over z_lo, x, y, core).
Axes of the slice: x: 4, y: 8, z: 8 (z_hi: 4, z_lo: 2; z = z_hi * 2 + z_lo), core: 2. Of those that a mesh axis runs over, the one named last changes fastest.
Arguments:
- tokens: bfloat16 [131072, 2304], P(('rep', 'fsdp')), may hold values from -24 to 24
- weight: bfloat16 [4, 2304, 1024], P('rep', 'fsdp'), may hold values from -0.125 to 0.125
- gain: bfloat16 [4, 2304], P('rep', 'fsdp'), may hold values from 0.25 to 1.75
- cotangent: bfloat16 [131072, 1024], P(('rep', 'fsdp')), may hold values from -6 to 6
- outer_delta: bfloat16 [4, 4, 2304, 1024], P('rep', None, 'fsdp'), may hold values from -6 to 6
- global_params: float32 [4, 2304, 1024], P(None, 'fsdp'), may hold values from -6 to 6
- momentum: float32 [4, 2304, 1024], P(None, 'fsdp'), may hold values from -6 to 6
- plan: int32 [4], replicated, may hold values 0 or 1
Outputs:
- layer_out: bfloat16 [131072, 1024], P(('rep', 'fsdp'))
- input_grad: bfloat16 [131072, 2304], P(('rep', 'fsdp'))
- weight_grad: float32 [4, 2304, 1024], P('rep', 'fsdp')
- gain_grad: float32 [4, 2304], P('rep', 'fsdp')
- new_params: float32 [4, 2304, 1024], P(None, 'fsdp')
- new_momentum: float32 [4, 2304, 1024], P(None, 'fsdp')
The draws below stay inside these ranges and needn't reach their ends.
All inputs are finite; a program needn't handle non-finite values.
Results may differ from the reference program's by a relative error of at most 0.008.
Values may be sent and summed in bfloat16 or wider, within the bound.
No kernel may reach another device: no remote copies, remote signals or barrier semaphores. Data moves between devices by JAX's collectives and lax.ppermute only.
A program may use at most 128 MiB of HBM per device.

```python
import math
import jax
import jax.numpy as jnp
from jax import lax

DW = 2304
KV = 1024
LB = 4
TOKENS = 32768
ROWS = 131072
N_REP = 4


def plant(values, key, least, high):
    shape = values.shape
    place = [jax.random.randint(jax.random.fold_in(key, axis), (), 0, shape[axis]) for axis in range(len(shape))]
    values = values.at[tuple(place)].set(least)
    longest = shape.index(max(shape))
    place[longest] = (place[longest] + 1) % shape[longest]
    return values.at[tuple(place)].set(high)


def spiked(result, key, source, target, blocks, factor):
    owner, partner = [(jnp.arange(result.shape[position]) // (result.shape[position] // blocks)).reshape([-1 if axis == position else 1 for axis in range(result.ndim)]) for position in (source, target)]
    chosen = jax.random.permutation(key, blocks)[partner]
    strong = (owner == chosen) | (owner == (partner + blocks // 2) % blocks)
    return jnp.where(strong, factor * result, result)


def level_of(stream_key, shape, pieces, low, largest):
    def one(dim, shards_of):
        draws = jax.random.uniform(jax.random.fold_in(jax.random.fold_in(stream_key, 6), dim), (shards_of,), jnp.float32, low / len(pieces), largest / len(pieces))
        return jnp.repeat(jnp.exp(draws), shape[dim] // shards_of).reshape((-1,) + (1,) * (len(shape) - dim - 1))

    factor_of = one(*pieces[0])
    for cut in pieces[1:]:
        factor_of = factor_of * one(*cut)
    return factor_of


def normal_values(key, dims, width, most, shards=(), kind=jnp.bfloat16):
    loudness = level_of(key, dims, shards, -0.22, 0.18) if shards else 1.0
    array = jax.random.normal(key, dims, jnp.float32) * width * loudness
    return jnp.minimum(jnp.maximum(array, -most), most).astype(kind)


def heavy_noise(rng, shape, scale, most, pieces, heavy, held_as=jnp.bfloat16):
    entries = scale * jax.random.normal(rng, shape, jnp.float32)
    if pieces:
        entries = entries * level_of(rng, shape, pieces, -0.22, 0.18)
    return jnp.clip(spiked(entries, jax.random.fold_in(rng, 3), *heavy), -most, most).astype(held_as)


def setup_inputs(seed: int = 0) -> dict:
    keys = jax.random.split(jax.random.key(seed), 9)
    tokens = heavy_noise(keys[0], (ROWS, DW), 1.0, 24.0, ((0, 512),), (0, 1, 256, 6.0))
    weight = normal_values(keys[1], (N_REP, DW, KV), DW ** -0.5, 0.125, ((0, 4), (1, 128)))
    gain = jnp.clip(1.0 + 0.15 * jax.random.normal(keys[2], (N_REP, DW), jnp.float32), 0.25, 1.75).astype(jnp.bfloat16)
    cotangent = normal_values(keys[3], (ROWS, KV), 1.0, 6.0, ((0, 512),))
    outer_delta = normal_values(keys[4], (N_REP, LB, DW, KV), 1.0, 6.0, ((0, 4), (2, 128)))
    global_params = normal_values(keys[5], (LB, DW, KV), 1.0, 6.0, ((1, 128),), jnp.float32)
    momentum = normal_values(keys[6], (LB, DW, KV), 1.0, 6.0, ((1, 128),), jnp.float32)
    plan = plant((jax.random.randint(keys[7], (LB,), 0, 4) < 3).astype(jnp.int32), jax.random.fold_in(keys[7], 1), 0, 1)
    return {"tokens": tokens, "weight": weight, "gain": gain, "cotangent": cotangent, "outer_delta": outer_delta, "global_params": global_params, "momentum": momentum, "plan": plan}


epsilon = 1e-06
outer_beta = 0.9
outer_rate = 0.7

def replica_pass(inputs):
    tokens, weight, gain, cotangent = inputs
    widened = tokens.astype(jnp.float32)
    recip = lax.rsqrt(lax.optimization_barrier(jnp.mean(widened * widened, -1, keepdims=True)) + epsilon)
    gain_wide = gain.astype(jnp.float32)
    normed = (widened * recip * gain_wide).astype(jnp.bfloat16)
    layer_out = jnp.dot(normed, weight, preferred_element_type=jnp.float32).astype(jnp.bfloat16)
    normed_grad = jnp.dot(cotangent, weight.T, preferred_element_type=jnp.float32)
    scaled = normed_grad * gain_wide
    inner = lax.optimization_barrier(jnp.mean(scaled * widened, -1, keepdims=True))
    input_grad = (recip * scaled - widened * recip * recip * recip * inner).astype(jnp.bfloat16)
    factor = 1.0 / math.sqrt(TOKENS)
    weight_grad = jnp.dot(normed.T, cotangent, preferred_element_type=jnp.float32) * factor
    gain_grad = lax.optimization_barrier(jnp.sum(normed_grad * widened * recip, 0)) * factor
    return (layer_out, input_grad, weight_grad, gain_grad)

def reference(tokens, weight, gain, cotangent, outer_delta, global_params, momentum, plan):
    stacked = (tokens.reshape(N_REP, TOKENS, DW), weight, gain, cotangent.reshape(N_REP, TOKENS, KV))
    layer_out, input_grad, weight_grad, gain_grad = lax.map(replica_pass, stacked)
    average = lax.optimization_barrier(jnp.sum(outer_delta.astype(jnp.float32), 0)) / N_REP
    chosen = (plan == 1)[:, None, None]
    moved = outer_beta * momentum + average
    new_momentum = jnp.where(chosen, moved, momentum)
    new_params = jnp.where(chosen, global_params - outer_rate * (average + outer_beta * moved), global_params)
    return (layer_out.reshape(N_REP * TOKENS, KV), input_grad.reshape(N_REP * TOKENS, DW), weight_grad, gain_grad, new_params, new_momentum)
```

```python
import functools
import math

import jax
import jax.numpy as jnp
from jax import lax
from jax.experimental import pallas as pl
from jax.experimental.pallas import tpu as pltpu
from jax.sharding import Mesh
from jax.sharding import PartitionSpec as P

epsilon = 1e-06
outer_beta = 0.9
outer_rate = 0.7
FSDP = ("z", "x", "y", "core")
ALL = ("rep",) + FSDP
f32, bf16 = jnp.float32, jnp.bfloat16


def outer_step(average, params, moment, chosen):
    moved = outer_beta * moment + average
    fresh_moment = jnp.where(chosen, moved, moment)
    fresh_params = jnp.where(chosen, params - outer_rate * (average + outer_beta * moved), params)
    return (fresh_params, fresh_moment)


def swap(values):
    return lax.ppermute(values, "core", [(0, 1), (1, 0)])


def exchange(values, axes):
    return lax.all_to_all(values, axes, split_axis=0, concat_axis=0, tiled=True)


def vmem(shape, index=None):
    return pl.BlockSpec(shape, index or (lambda *_: (0,) * len(shape)))


def params(mebibytes=40):
    return pltpu.CompilerParams(vmem_limit_bytes=mebibytes * 2**20)


def cost(flops, moved):
    return pl.CostEstimate(flops=flops, bytes_accessed=moved, transcendentals=0)


def row_recip(wide):
    return lax.rsqrt(jnp.mean(wide * wide, -1, keepdims=True) + epsilon)


def shrink_kernel(core_ref, tokens_ref, cot_ref, mine_ref, theirs_ref):
    half = mine_ref.shape[1]
    recip = row_recip(tokens_ref[...].astype(f32))
    here = pl.multiple_of(core_ref[0] * half, half)
    there = pl.multiple_of((1 - core_ref[0]) * half, half)
    mine_ref[...] = (cot_ref[:, pl.ds(here, half)].astype(f32) * recip).astype(bf16)
    theirs_ref[...] = (cot_ref[:, pl.ds(there, half)].astype(f32) * recip).astype(bf16)


def shrink(core, tokens, cotangent):
    rows, out = cotangent.shape
    half = jax.ShapeDtypeStruct((rows, out // 2), bf16)
    return pl.pallas_call(
        shrink_kernel,
        out_shape=(half, half),
        in_specs=[
            pl.BlockSpec(memory_space=pltpu.SMEM),
            pl.BlockSpec(memory_space=pltpu.VMEM),
            pl.BlockSpec(memory_space=pltpu.VMEM),
        ],
        out_specs=(pl.BlockSpec(memory_space=pltpu.VMEM),) * 2,
        compiler_params=params(),
        cost_estimate=cost(4 * tokens.size, 2 * tokens.size + 4 * cotangent.size),
        name="shrink",
    )(core, tokens, cotangent)


def partial_kernel(tokens_ref, others_ref, mine_ref, theirs_ref, out_ref):
    over_rows = (((0,), (0,)), ((), ()))
    first = lax.dot_general(
        tokens_ref[...], mine_ref[...], over_rows, preferred_element_type=f32
    )
    second = lax.dot_general(
        others_ref[...], theirs_ref[...], over_rows, preferred_element_type=f32
    )
    out_ref[...] = (first + second).astype(bf16)


def partial_product(tokens, others, mine, theirs):
    rows, width = tokens.shape
    half = mine.shape[1]
    step = width // 6
    return pl.pallas_call(
        partial_kernel,
        grid=(6,),
        out_shape=jax.ShapeDtypeStruct((width, half), bf16),
        in_specs=[
            pl.BlockSpec((rows, step), lambda i: (0, i)),
            pl.BlockSpec((rows, step), lambda i: (0, i)),
            vmem((rows, half)),
            vmem((rows, half)),
        ],
        out_specs=pl.BlockSpec((step, half), lambda i: (i, 0)),
        compiler_params=params(),
        cost_estimate=cost(4 * rows * width * half, 6 * rows * width),
        name="partial",
    )(tokens, others, mine, theirs)


def plane_kernel(parts_ref, out_ref):
    total = parts_ref[0].astype(f32)
    for i in range(1, parts_ref.shape[0]):
        total = total + parts_ref[i].astype(f32)
    own = out_ref.shape[1]
    for i in range(out_ref.shape[0]):
        out_ref[i] = total[i * own : (i + 1) * own].astype(bf16)


def plane_total(parts, owners):
    planes, rows, half = parts.shape
    return pl.pallas_call(
        plane_kernel,
        out_shape=jax.ShapeDtypeStruct((owners, rows // owners, half), bf16),
        compiler_params=params(),
        cost_estimate=cost(parts.size, 3 * parts.size),
        name="plane_total",
    )(parts)


def owner_kernel(factor, blocks_ref, weight_ref, gain_ref, weight_grad_ref, gain_grad_ref):
    half = blocks_ref.shape[2]
    dots = 0.0
    for core in range(2):
        total = blocks_ref[core].astype(f32)
        for column in range(1, blocks_ref.shape[0] // 2):
            total = total + blocks_ref[2 * column + core].astype(f32)
        total = total * factor
        columns = slice(core * half, (core + 1) * half)
        weight_grad_ref[0, :, columns] = total * gain_ref[...].astype(f32)
        dots = dots + jnp.sum(total * weight_ref[0, :, columns].astype(f32), -1, keepdims=True)
    gain_grad_ref[...] = dots


def owner_total(factor, blocks, weight, gain):
    own = weight.shape[1]
    return pl.pallas_call(
        functools.partial(owner_kernel, factor),
        out_shape=(
            jax.ShapeDtypeStruct(weight.shape, f32),
            jax.ShapeDtypeStruct((own, 1), f32),
        ),
        compiler_params=params(),
        cost_estimate=cost(blocks.size, 3 * blocks.size),
        name="owner_total",
    )(blocks, weight, gain)


def project_kernel(
    core_ref, tokens_ref, cot_ref, mine_ref, theirs_ref,
    layer_ref, grad_ref, whole, product, scaled,
):
    step = pl.program_id(0)
    columns, rows, half = mine_ref.shape
    band = whole.shape[0]
    group = 36
    for side, ref in enumerate((mine_ref, theirs_ref)):
        side_core = core_ref[0] if side == 0 else 1 - core_ref[0]
        place = pl.multiple_of(side_core * half, half)
        for plane in range(rows // group):
            piece = jnp.concatenate(
                [ref[y, plane * group : (plane + 1) * group, :] for y in range(columns)], 0
            )
            block = columns * group
            whole[plane * block : (plane + 1) * block, pl.ds(place, half)] = piece
    start = pl.multiple_of(step * band, 128)
    contribution = jnp.dot(
        tokens_ref[:, pl.ds(start, band)], whole[...], preferred_element_type=f32
    )
    scaled[step] = lax.dot_general(
        cot_ref[...], whole[...], (((1,), (1,)), ((), ())), preferred_element_type=f32
    )

    @pl.when(step == 0)
    def _():
        product[...] = contribution

    @pl.when(step == pl.num_programs(0) - 1)
    def _():
        width = tokens_ref.shape[1]
        wide = tokens_ref[...].astype(f32)
        recip = row_recip(wide)
        full = product[...] + contribution
        layer_ref[...] = (full * recip).astype(bf16)
        inner = jnp.sum(full * cot_ref[...].astype(f32), -1, keepdims=True) / width
        slope = recip * recip * recip * inner
        for part in range(2):
            lanes = slice(part * band, (part + 1) * band)
            grad = recip * scaled[part] - tokens_ref[:, lanes].astype(f32) * slope
            grad_ref[:, lanes] = grad.astype(bf16)


def project(core, tokens, cotangent, mine, theirs):
    rows, width = tokens.shape
    out = cotangent.shape[1]
    columns, per, half = mine.shape
    band = width // 2
    return pl.pallas_call(
        project_kernel,
        grid=(2,),
        out_shape=(
            jax.ShapeDtypeStruct((rows, out), bf16),
            jax.ShapeDtypeStruct((rows, width), bf16),
        ),
        in_specs=[
            pl.BlockSpec(memory_space=pltpu.SMEM),
            vmem((rows, width)),
            vmem((rows, out)),
            pl.BlockSpec((columns, per // 2, half), lambda i: (0, i, 0)),
            pl.BlockSpec((columns, per // 2, half), lambda i: (0, i, 0)),
        ],
        out_specs=(vmem((rows, out)), vmem((rows, width))),
        scratch_shapes=[
            pltpu.VMEM((band, out), bf16),
            pltpu.VMEM((rows, out), f32),
            pltpu.VMEM((2, rows, band), f32),
        ],
        compiler_params=params(48),
        cost_estimate=cost(4 * rows * width * out, 2 * width * out + 4 * rows * (width + out)),
        name="project",
    )(core, tokens, cotangent, mine, theirs)


def local(tokens, weight, gain, cotangent, outer_delta, global_params, momentum, plan):
    out = weight.shape[2]
    own, half = weight.shape[1], out // 2
    planes = lax.axis_size("z") * lax.axis_size("x")
    columns = lax.axis_size("y")
    core = lax.axis_index("core").astype(jnp.int32).reshape(1)
    replicas = lax.axis_size("rep")
    factor = 1.0 / math.sqrt(tokens.shape[0] * planes * columns * 2)

    summed = lax.psum(outer_delta[0], "rep")

    gain_column = gain.reshape(own, 1)
    scaled_weight = (weight[0].astype(f32) * gain_column.astype(f32)).astype(bf16)
    halves = jnp.stack([scaled_weight[:, :half], scaled_weight[:, half:]])
    spread = jnp.broadcast_to(halves[None], (planes, 2, own, half)).reshape(planes * 2, own, half)
    plane = exchange(spread, ("z", "x", "core")).reshape(planes * 2 * own, half)
    gathered = lax.all_gather(plane, "y", axis=0, tiled=True)

    others = swap(tokens)
    mine, theirs = shrink(core, tokens, cotangent)
    partial = partial_product(tokens, others, mine, swap(theirs))
    received = exchange(partial.reshape(planes, columns * 2 * own, half), ("z", "x"))
    plane_sum = plane_total(received, columns * 2)
    plane_sum, gathered, summed = lax.optimization_barrier((plane_sum, gathered, summed))
    blocks = exchange(plane_sum, ("y", "core"))
    weight_grad, gain_grad = owner_total(factor, blocks, weight, gain_column)

    gathered = gathered.reshape(columns, planes * 2 * own, half)
    layer_out, input_grad = project(core, tokens, cotangent, gathered, swap(gathered))

    chosen = (plan == 1)[:, None, None]
    new_params, new_momentum = outer_step(
        summed.astype(f32) / replicas, global_params, momentum, chosen
    )
    return (
        layer_out, input_grad, weight_grad, gain_grad.reshape(1, own), new_params, new_momentum
    )


def solution(mesh):
    fine = Mesh(mesh.devices.reshape(4, 2, 4, 8, 2), ALL)
    return jax.shard_map(
        local,
        mesh=fine,
        in_specs=(
            P(ALL, None),
            P("rep", FSDP, None),
            P("rep", FSDP),
            P(ALL, None),
            P("rep", None, FSDP, None),
            P(None, FSDP, None),
            P(None, FSDP, None),
            P(),
        ),
        out_specs=(
            P(ALL, None),
            P(ALL, None),
            P("rep", FSDP, None),
            P("rep", FSDP),
            P(None, FSDP, None),
            P(None, FSDP, None),
        ),
        check_vma=False,
    )
```

```python
import functools
import math

import jax
import jax.numpy as jnp
from jax import lax
from jax.experimental import pallas as pl
from jax.experimental.pallas import tpu as pltpu
from jax.sharding import Mesh
from jax.sharding import PartitionSpec as P

epsilon = 1e-06
outer_beta = 0.9
outer_rate = 0.7
FSDP = ("z", "x", "y", "core")
ALL = ("rep",) + FSDP
f32, bf16 = jnp.float32, jnp.bfloat16


def outer_step(average, params, moment, chosen):
    moved = outer_beta * moment + average
    fresh_moment = jnp.where(chosen, moved, moment)
    fresh_params = jnp.where(chosen, params - outer_rate * (average + outer_beta * moved), params)
    return (fresh_params, fresh_moment)


def swap(values):
    return lax.ppermute(values, "core", [(0, 1), (1, 0)])


def turn(values, by):
    count = lax.axis_size("y")
    return lax.ppermute(values, "y", [(i, (i + by) % count) for i in range(count)])


def cycle(values, by):
    count = lax.axis_size("rep")
    return lax.ppermute(values, "rep", [(i, (i + by) % count) for i in range(count)])


def exchange(values, axes):
    return lax.all_to_all(values, axes, split_axis=0, concat_axis=0, tiled=True)


def vmem(shape, index=None):
    return pl.BlockSpec(shape, index or (lambda *_: (0,) * len(shape)))


def params(mebibytes=40):
    return pltpu.CompilerParams(vmem_limit_bytes=mebibytes * 2**20)


def cost(flops, moved):
    return pl.CostEstimate(flops=flops, bytes_accessed=moved, transcendentals=0)


def row_recip(wide):
    return lax.rsqrt(jnp.mean(wide * wide, -1, keepdims=True) + epsilon)


def column_of(row):
    count = row.shape[1]
    shape = (count, count)
    same = lax.broadcasted_iota(jnp.int32, shape, 0) == lax.broadcasted_iota(jnp.int32, shape, 1)
    return jnp.sum(jnp.where(same, row, 0.0), 1, keepdims=True)


def row_of(column):
    count = column.shape[0]
    shape = (count, count)
    same = lax.broadcasted_iota(jnp.int32, shape, 0) == lax.broadcasted_iota(jnp.int32, shape, 1)
    return jnp.sum(jnp.where(same, column, 0.0), 0, keepdims=True)


def weigh_kernel(weight_ref, gain_ref, spread_ref):
    half = spread_ref.shape[2]
    gained = weight_ref[0].astype(f32) * column_of(gain_ref[...].astype(f32))
    gained = gained.astype(bf16)
    for i in range(spread_ref.shape[0]):
        side = i % 2
        spread_ref[i] = gained[:, side * half : (side + 1) * half]


def weigh(weight, gain, copies):
    _, own, out = weight.shape
    return pl.pallas_call(
        weigh_kernel,
        grid=(1,),
        out_shape=jax.ShapeDtypeStruct((2 * copies, own, out // 2), bf16),
        in_specs=[vmem(weight.shape), vmem(gain.shape)],
        out_specs=vmem((2 * copies, own, out // 2)),
        compiler_params=params(40),
        cost_estimate=cost(weight.size, 2 * copies * weight.size),
        name="weigh",
    )(weight, gain)


def stack_kernel(*refs):
    for i, ref in enumerate(refs[:-1]):
        refs[-1][i] = ref[...]


def stack_up(chunks):
    return pl.pallas_call(
        stack_kernel,
        out_shape=jax.ShapeDtypeStruct((len(chunks),) + chunks[0].shape, bf16),
        compiler_params=params(),
        cost_estimate=cost(0, 4 * len(chunks) * chunks[0].size),
        name="stack_up",
    )(*chunks)


def pack_kernel(parts_ref, out_ref):
    count = parts_ref.shape[0]
    for group in range(2):
        rows = [parts_ref[group * count // 2 + i] for i in range(count // 2)]
        span = out_ref.shape[0] // 2
        out_ref[group * span : (group + 1) * span, :] = jnp.concatenate(rows, 0)


def pack(parts):
    count, own, half = parts.shape
    return pl.pallas_call(
        pack_kernel,
        out_shape=jax.ShapeDtypeStruct((count * own, half), bf16),
        compiler_params=params(),
        cost_estimate=cost(0, 4 * parts.size),
        name="pack",
    )(parts)


def partial_kernel(
    core_ref, tokens_ref, others_ref, cot_ref, others_cot_ref, out_ref, mine, theirs
):
    half = mine.shape[1]
    step = out_ref.shape[0]
    place = pl.program_id(0)

    @pl.when(place == 0)
    def _():
        here = pl.ds(pl.multiple_of(core_ref[0] * half, half), half)
        for rows_ref, slopes_ref, shrunk in (
            (tokens_ref, cot_ref, mine), (others_ref, others_cot_ref, theirs)
        ):
            recip = row_recip(rows_ref[...].astype(f32))
            shrunk[...] = (slopes_ref[:, here].astype(f32) * recip).astype(bf16)

    over_rows = (((0,), (0,)), ((), ()))
    lanes = pl.ds(pl.multiple_of(place * step, 128), step)
    first = lax.dot_general(
        tokens_ref[:, lanes], mine[...], over_rows, preferred_element_type=f32
    )
    second = lax.dot_general(
        others_ref[:, lanes], theirs[...], over_rows, preferred_element_type=f32
    )
    out_ref[...] = (first + second).astype(bf16)


def partial_product(core, tokens, others, cotangent, others_cot):
    rows, width = tokens.shape
    out = cotangent.shape[1]
    step = width // 6
    return pl.pallas_call(
        partial_kernel,
        grid=(6,),
        out_shape=jax.ShapeDtypeStruct((width, out // 2), bf16),
        in_specs=[
            pl.BlockSpec(memory_space=pltpu.SMEM),
            vmem((rows, width)),
            vmem((rows, width)),
            vmem((rows, out)),
            vmem((rows, out)),
        ],
        out_specs=pl.BlockSpec((step, out // 2), lambda i: (i, 0)),
        scratch_shapes=[pltpu.VMEM((rows, out // 2), bf16)] * 2,
        compiler_params=params(),
        cost_estimate=cost(2 * rows * width * out, 6 * rows * width),
        name="partial",
    )(core, tokens, others, cotangent, others_cot)


def plane_kernel(parts_ref, out_ref):
    total = parts_ref[0].astype(f32)
    for i in range(1, parts_ref.shape[0]):
        total = total + parts_ref[i].astype(f32)
    own = out_ref.shape[1]
    for i in range(out_ref.shape[0]):
        out_ref[i] = total[i * own : (i + 1) * own].astype(bf16)


def plane_total(parts, owners):
    planes, rows, half = parts.shape
    return pl.pallas_call(
        plane_kernel,
        out_shape=jax.ShapeDtypeStruct((owners, rows // owners, half), bf16),
        compiler_params=params(),
        cost_estimate=cost(parts.size, 3 * parts.size),
        name="plane_total",
    )(parts)


def owner_kernel(factor, blocks_ref, weight_ref, gain_ref, weight_grad_ref, gain_grad_ref):
    half = blocks_ref.shape[2]
    gain = column_of(gain_ref[...].astype(f32))
    dots = 0.0
    for core in range(2):
        total = blocks_ref[core].astype(f32)
        for column in range(1, blocks_ref.shape[0] // 2):
            total = total + blocks_ref[2 * column + core].astype(f32)
        total = total * factor
        columns = slice(core * half, (core + 1) * half)
        weight_grad_ref[:, 0, columns] = total * gain
        dots = dots + jnp.sum(total * weight_ref[0, :, columns].astype(f32), -1, keepdims=True)
    gain_grad_ref[...] = row_of(dots)


def owner_total(factor, blocks, weight, gain):
    return pl.pallas_call(
        functools.partial(owner_kernel, factor),
        out_shape=(
            jax.ShapeDtypeStruct((weight.shape[1], 1, weight.shape[2]), f32),
            jax.ShapeDtypeStruct(gain.shape, f32),
        ),
        compiler_params=params(),
        cost_estimate=cost(blocks.size, 3 * blocks.size),
        name="owner_total",
    )(blocks, weight, gain)


def project_kernel(
    place_ref, tokens_ref, cot_ref, early_ref, late_ref, early_other_ref, late_other_ref,
    layer_ref, grad_ref, whole, product, scaled, stack,
):
    step = pl.program_id(0)
    columns, rows, half = stack.shape
    far = columns // 2
    band = whole.shape[0]
    at, core = place_ref[0], place_ref[1]
    for side, (first, last) in enumerate(
        ((early_ref, late_ref), (early_other_ref, late_other_ref))
    ):
        side_core = core if side == 0 else 1 - core
        stack[:far] = first[:far]
        stack[far] = last[...]
        stack[far + 1 :] = first[far:]
        place = pl.multiple_of(side_core * half, half)
        hops = []
        for y in range(columns):
            hops.append(jnp.where(at < y, at - y + columns, at - y))
        for plane in range(rows // 36):
            span = slice(plane * 36, (plane + 1) * 36)
            piece = jnp.concatenate([stack[hop, span, :] for hop in hops], 0)
            block = columns * 36
            whole[plane * block : (plane + 1) * block, pl.ds(place, half)] = piece
    start = pl.multiple_of(step * band, 128)
    contribution = jnp.dot(
        tokens_ref[:, pl.ds(start, band)], whole[...], preferred_element_type=f32
    )
    scaled[step] = lax.dot_general(
        cot_ref[...], whole[...], (((1,), (1,)), ((), ())), preferred_element_type=f32
    )

    @pl.when(step == 0)
    def _():
        product[...] = contribution

    @pl.when(step == pl.num_programs(0) - 1)
    def _():
        width = tokens_ref.shape[1]
        wide = tokens_ref[...].astype(f32)
        recip = row_recip(wide)
        full = product[...] + contribution
        layer_ref[...] = (full * recip).astype(bf16)
        inner = jnp.sum(full * cot_ref[...].astype(f32), -1, keepdims=True) / width
        slope = recip * recip * recip * inner
        for part in range(2):
            lanes = slice(part * band, (part + 1) * band)
            grad = recip * scaled[part] - tokens_ref[:, lanes].astype(f32) * slope
            grad_ref[:, lanes] = grad.astype(bf16)


def project(place, tokens, cotangent, early, late, early_other, late_other):
    rows, width = tokens.shape
    out = cotangent.shape[1]
    first, per, half = early.shape
    band = width // 2
    return pl.pallas_call(
        project_kernel,
        grid=(2,),
        out_shape=(
            jax.ShapeDtypeStruct((rows, out), bf16),
            jax.ShapeDtypeStruct((rows, width), bf16),
        ),
        in_specs=[
            pl.BlockSpec(memory_space=pltpu.SMEM),
            vmem((rows, width)),
            vmem((rows, out)),
            pl.BlockSpec((first, per // 2, half), lambda i: (0, i, 0)),
            pl.BlockSpec((per // 2, half), lambda i: (i, 0)),
            pl.BlockSpec((first, per // 2, half), lambda i: (0, i, 0)),
            pl.BlockSpec((per // 2, half), lambda i: (i, 0)),
        ],
        out_specs=(vmem((rows, out)), vmem((rows, width))),
        scratch_shapes=[
            pltpu.VMEM((band, out), bf16),
            pltpu.VMEM((rows, out), f32),
            pltpu.VMEM((2, rows, band), f32),
            pltpu.VMEM((first + 1, per // 2, half), bf16),
        ],
        compiler_params=params(48),
        cost_estimate=cost(4 * rows * width * out, 2 * width * out + 4 * rows * (width + out)),
        name="project",
    )(place, tokens, cotangent, early, late, early_other, late_other)


def local(tokens, weight, gain, cotangent, outer_delta, global_params, momentum, plan):
    out = weight.shape[2]
    own, half = weight.shape[1], out // 2
    planes = lax.axis_size("z") * lax.axis_size("x")
    columns = lax.axis_size("y")
    place = jnp.stack([lax.axis_index("y"), lax.axis_index("core")]).astype(jnp.int32)
    core = place[1:]
    replicas = lax.axis_size("rep")
    factor = 1.0 / math.sqrt(tokens.shape[0] * planes * columns * 2)
    after = lax.optimization_barrier

    spread = weigh(weight, gain, planes)
    plane_parts = exchange(spread, ("z", "x", "core"))

    partial = partial_product(core, tokens, swap(tokens), cotangent, swap(cotangent))
    plane = pack(plane_parts)
    received = exchange(partial.reshape(planes, columns * 2 * own, half), ("z", "x"))

    up, down = [plane], [plane]
    for hop in range(1, columns // 2 + 1):
        if hop == columns // 2:
            above, received, below = after((up[-1], received, down[-1]))
            plane_sum = plane_total(received, columns * 2)
            blocks = exchange(plane_sum, ("y", "core"))
            early = stack_up(up + down[:0:-1])
            early_other = swap(early)
            late = turn(above, 1)
        else:
            up.append(turn(up[-1], 1))
            down.append(turn(down[-1], -1))
    weight_grad, gain_grad = owner_total(factor, blocks, weight, gain)
    weight_grad = weight_grad.transpose(1, 0, 2)

    delta, plane_sum = after((outer_delta[0], plane_sum))
    before, behind = cycle(delta, 1), cycle(delta, -1)
    across = cycle(before, 1)
    summed = (delta.astype(f32) + across.astype(f32)) + (before.astype(f32) + behind.astype(f32))

    layer_out, input_grad = project(
        place, tokens, cotangent, early, late, early_other, swap(late)
    )

    chosen = (plan == 1)[:, None, None]
    new_params, new_momentum = outer_step(
        summed / replicas, global_params, momentum, chosen
    )
    return (
        layer_out, input_grad, weight_grad, gain_grad, new_params, new_momentum
    )


def solution(mesh):
    fine = Mesh(mesh.devices.reshape(4, 2, 4, 8, 2), ALL)
    return jax.shard_map(
        local,
        mesh=fine,
        in_specs=(
            P(ALL, None),
            P("rep", FSDP, None),
            P("rep", FSDP),
            P(ALL, None),
            P("rep", None, FSDP, None),
            P(None, FSDP, None),
            P(None, FSDP, None),
            P(),
        ),
        out_specs=(
            P(ALL, None),
            P(ALL, None),
            P("rep", FSDP, None),
            P("rep", FSDP),
            P(None, FSDP, None),
            P(None, FSDP, None),
        ),
        check_vma=False,
    )
```

```python
import functools
import math

import jax
import jax.numpy as jnp
from jax import lax
from jax.experimental import pallas as pl
from jax.experimental.pallas import tpu as pltpu
from jax.sharding import Mesh
from jax.sharding import PartitionSpec as P

epsilon = 1e-06
outer_beta = 0.9
outer_rate = 0.7
FSDP = ("z", "x", "y", "core")
ALL = ("rep",) + FSDP
f32, bf16 = jnp.float32, jnp.bfloat16


def outer_step(average, params, moment, chosen):
    moved = outer_beta * moment + average
    fresh_moment = jnp.where(chosen, moved, moment)
    fresh_params = jnp.where(chosen, params - outer_rate * (average + outer_beta * moved), params)
    return (fresh_params, fresh_moment)


def swap(values):
    return lax.ppermute(values, "core", [(0, 1), (1, 0)])


def turn(values, by):
    count = lax.axis_size("y")
    return lax.ppermute(values, "y", [(i, (i + by) % count) for i in range(count)])


def partner(values, partners):
    return lax.ppermute(values, "rep", list(enumerate(partners)))


def exchange(values, axes):
    return lax.all_to_all(values, axes, split_axis=0, concat_axis=0, tiled=True)


def vmem(shape, index=None):
    return pl.BlockSpec(shape, index or (lambda *_: (0,) * len(shape)))


def params(mebibytes=40):
    return pltpu.CompilerParams(vmem_limit_bytes=mebibytes * 2**20)


def cost(flops, moved):
    return pl.CostEstimate(flops=flops, bytes_accessed=moved, transcendentals=0)


def row_recip(wide):
    return lax.rsqrt(jnp.mean(wide * wide, -1, keepdims=True) + epsilon)


def column_of(row):
    count = row.shape[1]
    shape = (count, count)
    same = lax.broadcasted_iota(jnp.int32, shape, 0) == lax.broadcasted_iota(jnp.int32, shape, 1)
    return jnp.sum(jnp.where(same, row, 0.0), 1, keepdims=True)


def row_of(column):
    count = column.shape[0]
    shape = (count, count)
    same = lax.broadcasted_iota(jnp.int32, shape, 0) == lax.broadcasted_iota(jnp.int32, shape, 1)
    return jnp.sum(jnp.where(same, column, 0.0), 0, keepdims=True)


def weigh_kernel(weight_ref, gain_ref, spread_ref):
    half = spread_ref.shape[2]
    gained = weight_ref[0].astype(f32) * column_of(gain_ref[...].astype(f32))
    gained = gained.astype(bf16)
    for i in range(spread_ref.shape[0]):
        side = i % 2
        spread_ref[i] = gained[:, side * half : (side + 1) * half]


def weigh(weight, gain, copies):
    _, own, out = weight.shape
    return pl.pallas_call(
        weigh_kernel,
        grid=(1,),
        out_shape=jax.ShapeDtypeStruct((2 * copies, own, out // 2), bf16),
        in_specs=[vmem(weight.shape), vmem(gain.shape)],
        out_specs=vmem((2 * copies, own, out // 2)),
        compiler_params=params(40),
        cost_estimate=cost(weight.size, 2 * copies * weight.size),
        name="weigh",
    )(weight, gain)


def stack_kernel(*refs):
    for i, ref in enumerate(refs[:-1]):
        refs[-1][i] = ref[...]


def stack_up(chunks):
    return pl.pallas_call(
        stack_kernel,
        out_shape=jax.ShapeDtypeStruct((len(chunks),) + chunks[0].shape, bf16),
        compiler_params=params(),
        cost_estimate=cost(0, 4 * len(chunks) * chunks[0].size),
        name="stack_up",
    )(*chunks)


def pack_kernel(parts_ref, out_ref):
    count = parts_ref.shape[0]
    for group in range(2):
        rows = [parts_ref[group * count // 2 + i] for i in range(count // 2)]
        span = out_ref.shape[0] // 2
        out_ref[group * span : (group + 1) * span, :] = jnp.concatenate(rows, 0)


def pack(parts):
    count, own, half = parts.shape
    return pl.pallas_call(
        pack_kernel,
        out_shape=jax.ShapeDtypeStruct((count * own, half), bf16),
        compiler_params=params(),
        cost_estimate=cost(0, 4 * parts.size),
        name="pack",
    )(parts)


def partial_kernel(
    core_ref, tokens_ref, others_ref, cot_ref, others_cot_ref, out_ref, mine, theirs
):
    half = mine.shape[1]
    step = out_ref.shape[0]
    place = pl.program_id(0)

    @pl.when(place == 0)
    def _():
        here = pl.ds(pl.multiple_of(core_ref[0] * half, half), half)
        for rows_ref, slopes_ref, shrunk in (
            (tokens_ref, cot_ref, mine), (others_ref, others_cot_ref, theirs)
        ):
            recip = row_recip(rows_ref[...].astype(f32))
            shrunk[...] = (slopes_ref[:, here].astype(f32) * recip).astype(bf16)

    over_rows = (((0,), (0,)), ((), ()))
    lanes = pl.ds(pl.multiple_of(place * step, 128), step)
    first = lax.dot_general(
        tokens_ref[:, lanes], mine[...], over_rows, preferred_element_type=f32
    )
    second = lax.dot_general(
        others_ref[:, lanes], theirs[...], over_rows, preferred_element_type=f32
    )
    out_ref[...] = (first + second).astype(bf16)


def partial_product(core, tokens, others, cotangent, others_cot):
    rows, width = tokens.shape
    out = cotangent.shape[1]
    step = width // 6
    return pl.pallas_call(
        partial_kernel,
        grid=(6,),
        out_shape=jax.ShapeDtypeStruct((width, out // 2), bf16),
        in_specs=[
            pl.BlockSpec(memory_space=pltpu.SMEM),
            vmem((rows, width)),
            vmem((rows, width)),
            vmem((rows, out)),
            vmem((rows, out)),
        ],
        out_specs=pl.BlockSpec((step, out // 2), lambda i: (i, 0)),
        scratch_shapes=[pltpu.VMEM((rows, out // 2), bf16)] * 2,
        compiler_params=params(),
        cost_estimate=cost(2 * rows * width * out, 6 * rows * width),
        name="partial",
    )(core, tokens, others, cotangent, others_cot)


def plane_kernel(parts_ref, out_ref):
    total = parts_ref[0].astype(f32)
    for i in range(1, parts_ref.shape[0]):
        total = total + parts_ref[i].astype(f32)
    own = out_ref.shape[1]
    for i in range(out_ref.shape[0]):
        out_ref[i] = total[i * own : (i + 1) * own].astype(bf16)


def plane_total(parts, owners):
    planes, rows, half = parts.shape
    return pl.pallas_call(
        plane_kernel,
        out_shape=jax.ShapeDtypeStruct((owners, rows // owners, half), bf16),
        compiler_params=params(),
        cost_estimate=cost(parts.size, 3 * parts.size),
        name="plane_total",
    )(parts)


def owner_kernel(factor, blocks_ref, weight_ref, gain_ref, weight_grad_ref, gain_grad_ref):
    half = blocks_ref.shape[2]
    gain = column_of(gain_ref[...].astype(f32))
    dots = 0.0
    for core in range(2):
        total = blocks_ref[core].astype(f32)
        for column in range(1, blocks_ref.shape[0] // 2):
            total = total + blocks_ref[2 * column + core].astype(f32)
        total = total * factor
        columns = slice(core * half, (core + 1) * half)
        weight_grad_ref[:, 0, columns] = total * gain
        dots = dots + jnp.sum(total * weight_ref[0, :, columns].astype(f32), -1, keepdims=True)
    gain_grad_ref[...] = row_of(dots)


def owner_total(factor, blocks, weight, gain):
    return pl.pallas_call(
        functools.partial(owner_kernel, factor),
        out_shape=(
            jax.ShapeDtypeStruct((weight.shape[1], 1, weight.shape[2]), f32),
            jax.ShapeDtypeStruct(gain.shape, f32),
        ),
        compiler_params=params(),
        cost_estimate=cost(blocks.size, 3 * blocks.size),
        name="owner_total",
    )(blocks, weight, gain)


def project_kernel(
    place_ref, tokens_ref, cot_ref, early_ref, late_ref, early_other_ref, late_other_ref,
    layer_ref, grad_ref, whole, product, scaled, stack,
):
    step = pl.program_id(0)
    columns, rows, half = stack.shape
    far = columns // 2
    band = whole.shape[0]
    at, core = place_ref[0], place_ref[1]
    for side, (first, last) in enumerate(
        ((early_ref, late_ref), (early_other_ref, late_other_ref))
    ):
        side_core = core if side == 0 else 1 - core
        stack[:far] = first[:far]
        stack[far] = last[...]
        stack[far + 1 :] = first[far:]
        place = pl.multiple_of(side_core * half, half)
        hops = []
        for y in range(columns):
            hops.append(jnp.where(at < y, at - y + columns, at - y))
        for plane in range(rows // 36):
            span = slice(plane * 36, (plane + 1) * 36)
            piece = jnp.concatenate([stack[hop, span, :] for hop in hops], 0)
            block = columns * 36
            whole[plane * block : (plane + 1) * block, pl.ds(place, half)] = piece
    start = pl.multiple_of(step * band, 128)
    contribution = jnp.dot(
        tokens_ref[:, pl.ds(start, band)], whole[...], preferred_element_type=f32
    )
    scaled[step] = lax.dot_general(
        cot_ref[...], whole[...], (((1,), (1,)), ((), ())), preferred_element_type=f32
    )

    @pl.when(step == 0)
    def _():
        product[...] = contribution

    @pl.when(step == pl.num_programs(0) - 1)
    def _():
        width = tokens_ref.shape[1]
        wide = tokens_ref[...].astype(f32)
        recip = row_recip(wide)
        full = product[...] + contribution
        layer_ref[...] = (full * recip).astype(bf16)
        inner = jnp.sum(full * cot_ref[...].astype(f32), -1, keepdims=True) / width
        slope = recip * recip * recip * inner
        for part in range(2):
            lanes = slice(part * band, (part + 1) * band)
            grad = recip * scaled[part] - tokens_ref[:, lanes].astype(f32) * slope
            grad_ref[:, lanes] = grad.astype(bf16)


def project(place, tokens, cotangent, early, late, early_other, late_other):
    rows, width = tokens.shape
    out = cotangent.shape[1]
    first, per, half = early.shape
    band = width // 2
    return pl.pallas_call(
        project_kernel,
        grid=(2,),
        out_shape=(
            jax.ShapeDtypeStruct((rows, out), bf16),
            jax.ShapeDtypeStruct((rows, width), bf16),
        ),
        in_specs=[
            pl.BlockSpec(memory_space=pltpu.SMEM),
            vmem((rows, width)),
            vmem((rows, out)),
            pl.BlockSpec((first, per // 2, half), lambda i: (0, i, 0)),
            pl.BlockSpec((per // 2, half), lambda i: (i, 0)),
            pl.BlockSpec((first, per // 2, half), lambda i: (0, i, 0)),
            pl.BlockSpec((per // 2, half), lambda i: (i, 0)),
        ],
        out_specs=(vmem((rows, out)), vmem((rows, width))),
        scratch_shapes=[
            pltpu.VMEM((band, out), bf16),
            pltpu.VMEM((rows, out), f32),
            pltpu.VMEM((2, rows, band), f32),
            pltpu.VMEM((first + 1, per // 2, half), bf16),
        ],
        compiler_params=params(48),
        cost_estimate=cost(4 * rows * width * out, 2 * width * out + 4 * rows * (width + out)),
        name="project",
    )(place, tokens, cotangent, early, late, early_other, late_other)


def local(tokens, weight, gain, cotangent, outer_delta, global_params, momentum, plan):
    out = weight.shape[2]
    own, half = weight.shape[1], out // 2
    planes = lax.axis_size("z") * lax.axis_size("x")
    columns = lax.axis_size("y")
    place = jnp.stack([lax.axis_index("y"), lax.axis_index("core")]).astype(jnp.int32)
    core = place[1:]
    replicas = lax.axis_size("rep")
    factor = 1.0 / math.sqrt(tokens.shape[0] * planes * columns * 2)
    after = lax.optimization_barrier

    spread = weigh(weight, gain, planes)
    plane_parts = exchange(spread, ("z", "x", "core"))

    ready_tokens, ready_cot, _ = after((tokens, cotangent, spread))
    partial = partial_product(core, tokens, swap(ready_tokens), cotangent, swap(ready_cot))
    plane = pack(plane_parts)
    received = exchange(partial.reshape(planes, columns * 2 * own, half), ("z", "x"))

    up, down = [plane], [plane]
    for hop in range(1, columns // 2 + 1):
        if hop == columns // 2:
            above, received, below = after((up[-1], received, down[-1]))
            plane_sum = plane_total(received, columns * 2)
            blocks = exchange(plane_sum, ("y", "core"))
            early = stack_up(up + down[:0:-1])
            early_other = swap(early)
            late = turn(above, 1)
        else:
            up.append(turn(up[-1], 1))
            down.append(turn(down[-1], -1))

    delta, plane_sum = after((outer_delta[0], plane_sum))
    pair = (delta.astype(f32) + partner(delta, (1, 0, 3, 2)).astype(f32)).astype(bf16)
    pair, late = after((pair, late))
    other_pair = partner(pair, (3, 2, 1, 0))

    layer_out, input_grad = project(
        place, tokens, cotangent, early, late, early_other, swap(late)
    )

    layer_out, other_pair, blocks = after((layer_out, other_pair, blocks))
    summed = pair.astype(f32) + other_pair.astype(f32)
    weight_grad, gain_grad = owner_total(factor, blocks, weight, gain)
    weight_grad = weight_grad.transpose(1, 0, 2)

    chosen = (plan == 1)[:, None, None]
    new_params, new_momentum = outer_step(
        summed / replicas, global_params, momentum, chosen
    )
    return (
        layer_out, input_grad, weight_grad, gain_grad, new_params, new_momentum
    )


def solution(mesh):
    fine = Mesh(mesh.devices.reshape(4, 2, 4, 8, 2), ALL)
    return jax.shard_map(
        local,
        mesh=fine,
        in_specs=(
            P(ALL, None),
            P("rep", FSDP, None),
            P("rep", FSDP),
            P(ALL, None),
            P("rep", None, FSDP, None),
            P(None, FSDP, None),
            P(None, FSDP, None),
            P(),
        ),
        out_specs=(
            P(ALL, None),
            P(ALL, None),
            P("rep", FSDP, None),
            P("rep", FSDP),
            P(None, FSDP, None),
            P(None, FSDP, None),
        ),
        check_vma=False,
    )
```

```python
import functools
import math

import jax
import jax.numpy as jnp
from jax import lax
from jax.experimental import pallas as pl
from jax.experimental.pallas import tpu as pltpu
from jax.sharding import Mesh
from jax.sharding import PartitionSpec as P

epsilon = 1e-06
outer_beta = 0.9
outer_rate = 0.7
FSDP = ("z", "x", "y", "core")
ALL = ("rep",) + FSDP
f32, bf16 = jnp.float32, jnp.bfloat16


def outer_step(average, params, moment, chosen):
    moved = outer_beta * moment + average
    fresh_moment = jnp.where(chosen, moved, moment)
    fresh_params = jnp.where(chosen, params - outer_rate * (average + outer_beta * moved), params)
    return (fresh_params, fresh_moment)


def swap(values):
    return lax.ppermute(values, "core", [(0, 1), (1, 0)])


def turn(values, by):
    count = lax.axis_size("y")
    return lax.ppermute(values, "y", [(i, (i + by) % count) for i in range(count)])


def partner(values, partners):
    return lax.ppermute(values, "rep", list(enumerate(partners)))


def exchange(values, axes):
    return lax.all_to_all(values, axes, split_axis=0, concat_axis=0, tiled=True)


def vmem(shape, index=None):
    return pl.BlockSpec(shape, index or (lambda *_: (0,) * len(shape)))


def params(mebibytes=40):
    return pltpu.CompilerParams(vmem_limit_bytes=mebibytes * 2**20)


def cost(flops, moved):
    return pl.CostEstimate(flops=flops, bytes_accessed=moved, transcendentals=0)


def row_recip(wide):
    return lax.rsqrt(jnp.mean(wide * wide, -1, keepdims=True) + epsilon)


def column_of(row):
    count = row.shape[1]
    shape = (count, count)
    same = lax.broadcasted_iota(jnp.int32, shape, 0) == lax.broadcasted_iota(jnp.int32, shape, 1)
    return jnp.sum(jnp.where(same, row, 0.0), 1, keepdims=True)


def row_of(column):
    count = column.shape[0]
    shape = (count, count)
    same = lax.broadcasted_iota(jnp.int32, shape, 0) == lax.broadcasted_iota(jnp.int32, shape, 1)
    return jnp.sum(jnp.where(same, column, 0.0), 0, keepdims=True)


def weigh_kernel(weight_ref, gain_ref, spread_ref):
    half = spread_ref.shape[2]
    gained = weight_ref[0].astype(f32) * column_of(gain_ref[...].astype(f32))
    gained = gained.astype(bf16)
    for i in range(spread_ref.shape[0]):
        side = i % 2
        spread_ref[i] = gained[:, side * half : (side + 1) * half]


def weigh(weight, gain, copies):
    _, own, out = weight.shape
    return pl.pallas_call(
        weigh_kernel,
        grid=(1,),
        out_shape=jax.ShapeDtypeStruct((2 * copies, own, out // 2), bf16),
        in_specs=[vmem(weight.shape), vmem(gain.shape)],
        out_specs=vmem((2 * copies, own, out // 2)),
        compiler_params=params(40),
        cost_estimate=cost(weight.size, 2 * copies * weight.size),
        name="weigh",
    )(weight, gain)


def stack_kernel(*refs):
    for i, ref in enumerate(refs[:-1]):
        refs[-1][i] = ref[...]


def stack_up(chunks):
    return pl.pallas_call(
        stack_kernel,
        out_shape=jax.ShapeDtypeStruct((len(chunks),) + chunks[0].shape, bf16),
        compiler_params=params(),
        cost_estimate=cost(0, 4 * len(chunks) * chunks[0].size),
        name="stack_up",
    )(*chunks)


def pack_kernel(parts_ref, out_ref):
    count = parts_ref.shape[0]
    for group in range(2):
        rows = [parts_ref[group * count // 2 + i] for i in range(count // 2)]
        span = out_ref.shape[0] // 2
        out_ref[group * span : (group + 1) * span, :] = jnp.concatenate(rows, 0)


def pack(parts):
    count, own, half = parts.shape
    return pl.pallas_call(
        pack_kernel,
        out_shape=jax.ShapeDtypeStruct((count * own, half), bf16),
        compiler_params=params(),
        cost_estimate=cost(0, 4 * parts.size),
        name="pack",
    )(parts)


def partial_kernel(
    core_ref, tokens_ref, others_ref, cot_ref, others_cot_ref, out_ref, mine, theirs
):
    half = mine.shape[1]
    step = out_ref.shape[0]
    place = pl.program_id(0)

    @pl.when(place == 0)
    def _():
        here = pl.ds(pl.multiple_of(core_ref[0] * half, half), half)
        for rows_ref, slopes_ref, shrunk in (
            (tokens_ref, cot_ref, mine), (others_ref, others_cot_ref, theirs)
        ):
            recip = row_recip(rows_ref[...].astype(f32))
            shrunk[...] = (slopes_ref[:, here].astype(f32) * recip).astype(bf16)

    over_rows = (((0,), (0,)), ((), ()))
    lanes = pl.ds(pl.multiple_of(place * step, 128), step)
    first = lax.dot_general(
        tokens_ref[:, lanes], mine[...], over_rows, preferred_element_type=f32
    )
    second = lax.dot_general(
        others_ref[:, lanes], theirs[...], over_rows, preferred_element_type=f32
    )
    out_ref[...] = (first + second).astype(bf16)


def partial_product(core, tokens, others, cotangent, others_cot):
    rows, width = tokens.shape
    out = cotangent.shape[1]
    step = width // 3
    return pl.pallas_call(
        partial_kernel,
        grid=(3,),
        out_shape=jax.ShapeDtypeStruct((width, out // 2), bf16),
        in_specs=[
            pl.BlockSpec(memory_space=pltpu.SMEM),
            vmem((rows, width)),
            vmem((rows, width)),
            vmem((rows, out)),
            vmem((rows, out)),
        ],
        out_specs=pl.BlockSpec((step, out // 2), lambda i: (i, 0)),
        scratch_shapes=[pltpu.VMEM((rows, out // 2), bf16)] * 2,
        compiler_params=params(),
        cost_estimate=cost(2 * rows * width * out, 6 * rows * width),
        name="partial",
    )(core, tokens, others, cotangent, others_cot)


def plane_kernel(parts_ref, out_ref):
    total = parts_ref[0].astype(f32)
    for i in range(1, parts_ref.shape[0]):
        total = total + parts_ref[i].astype(f32)
    own = out_ref.shape[1]
    for i in range(out_ref.shape[0]):
        out_ref[i] = total[i * own : (i + 1) * own].astype(bf16)


def plane_total(parts, owners):
    planes, rows, half = parts.shape
    return pl.pallas_call(
        plane_kernel,
        out_shape=jax.ShapeDtypeStruct((owners, rows // owners, half), bf16),
        compiler_params=params(),
        cost_estimate=cost(parts.size, 3 * parts.size),
        name="plane_total",
    )(parts)


def owner_kernel(factor, blocks_ref, weight_ref, gain_ref, weight_grad_ref, gain_grad_ref):
    half = blocks_ref.shape[2]
    gain = column_of(gain_ref[...].astype(f32))
    dots = 0.0
    for core in range(2):
        total = blocks_ref[core].astype(f32)
        for column in range(1, blocks_ref.shape[0] // 2):
            total = total + blocks_ref[2 * column + core].astype(f32)
        total = total * factor
        columns = slice(core * half, (core + 1) * half)
        weight_grad_ref[:, 0, columns] = total * gain
        dots = dots + jnp.sum(total * weight_ref[0, :, columns].astype(f32), -1, keepdims=True)
    gain_grad_ref[...] = row_of(dots)


def owner_total(factor, blocks, weight, gain):
    return pl.pallas_call(
        functools.partial(owner_kernel, factor),
        out_shape=(
            jax.ShapeDtypeStruct((weight.shape[1], 1, weight.shape[2]), f32),
            jax.ShapeDtypeStruct(gain.shape, f32),
        ),
        compiler_params=params(),
        cost_estimate=cost(blocks.size, 3 * blocks.size),
        name="owner_total",
    )(blocks, weight, gain)


def project_kernel(
    place_ref, tokens_ref, cot_ref, early_ref, late_ref, early_other_ref, late_other_ref,
    layer_ref, grad_ref, whole, product, scaled, stack,
):
    step = pl.program_id(0)
    columns, rows, half = stack.shape
    far = columns // 2
    band = whole.shape[0]
    at, core = place_ref[0], place_ref[1]
    for side, (first, last) in enumerate(
        ((early_ref, late_ref), (early_other_ref, late_other_ref))
    ):
        side_core = core if side == 0 else 1 - core
        stack[:far] = first[:far]
        stack[far] = last[...]
        stack[far + 1 :] = first[far:]
        place = pl.multiple_of(side_core * half, half)
        hops = []
        for y in range(columns):
            hops.append(jnp.where(at < y, at - y + columns, at - y))
        for plane in range(rows // 36):
            span = slice(plane * 36, (plane + 1) * 36)
            piece = jnp.concatenate([stack[hop, span, :] for hop in hops], 0)
            block = columns * 36
            whole[plane * block : (plane + 1) * block, pl.ds(place, half)] = piece
    start = pl.multiple_of(step * band, 128)
    contribution = jnp.dot(
        tokens_ref[:, pl.ds(start, band)], whole[...], preferred_element_type=f32
    )
    scaled[step] = lax.dot_general(
        cot_ref[...], whole[...], (((1,), (1,)), ((), ())), preferred_element_type=f32
    )

    @pl.when(step == 0)
    def _():
        product[...] = contribution

    @pl.when(step == pl.num_programs(0) - 1)
    def _():
        width = tokens_ref.shape[1]
        wide = tokens_ref[...].astype(f32)
        recip = row_recip(wide)
        full = product[...] + contribution
        layer_ref[...] = (full * recip).astype(bf16)
        inner = jnp.sum(full * cot_ref[...].astype(f32), -1, keepdims=True) / width
        slope = recip * recip * recip * inner
        for part in range(2):
            lanes = slice(part * band, (part + 1) * band)
            grad = recip * scaled[part] - tokens_ref[:, lanes].astype(f32) * slope
            grad_ref[:, lanes] = grad.astype(bf16)


def project(place, tokens, cotangent, early, late, early_other, late_other):
    rows, width = tokens.shape
    out = cotangent.shape[1]
    first, per, half = early.shape
    band = width // 2
    return pl.pallas_call(
        project_kernel,
        grid=(2,),
        out_shape=(
            jax.ShapeDtypeStruct((rows, out), bf16),
            jax.ShapeDtypeStruct((rows, width), bf16),
        ),
        in_specs=[
            pl.BlockSpec(memory_space=pltpu.SMEM),
            vmem((rows, width)),
            vmem((rows, out)),
            pl.BlockSpec((first, per // 2, half), lambda i: (0, i, 0)),
            pl.BlockSpec((per // 2, half), lambda i: (i, 0)),
            pl.BlockSpec((first, per // 2, half), lambda i: (0, i, 0)),
            pl.BlockSpec((per // 2, half), lambda i: (i, 0)),
        ],
        out_specs=(vmem((rows, out)), vmem((rows, width))),
        scratch_shapes=[
            pltpu.VMEM((band, out), bf16),
            pltpu.VMEM((rows, out), f32),
            pltpu.VMEM((2, rows, band), f32),
            pltpu.VMEM((first + 1, per // 2, half), bf16),
        ],
        compiler_params=params(48),
        cost_estimate=cost(4 * rows * width * out, 2 * width * out + 4 * rows * (width + out)),
        name="project",
    )(place, tokens, cotangent, early, late, early_other, late_other)


def local(tokens, weight, gain, cotangent, outer_delta, global_params, momentum, plan):
    out = weight.shape[2]
    own, half = weight.shape[1], out // 2
    planes = lax.axis_size("z") * lax.axis_size("x")
    columns = lax.axis_size("y")
    place = jnp.stack([lax.axis_index("y"), lax.axis_index("core")]).astype(jnp.int32)
    core = place[1:]
    replicas = lax.axis_size("rep")
    factor = 1.0 / math.sqrt(tokens.shape[0] * planes * columns * 2)
    after = lax.optimization_barrier

    spread = weigh(weight, gain, planes)
    plane_parts = exchange(spread, ("z", "x", "core"))

    ready_tokens, ready_cot, _ = after((tokens, cotangent, spread))
    partial = partial_product(core, tokens, swap(ready_tokens), cotangent, swap(ready_cot))
    plane = pack(plane_parts)
    received = exchange(partial.reshape(planes, columns * 2 * own, half), ("z", "x"))

    up, down = [plane], [plane]
    for hop in range(1, columns // 2 + 1):
        if hop == columns // 2:
            above, received, below = after((up[-1], received, down[-1]))
            plane_sum = plane_total(received, columns * 2)
            blocks = exchange(plane_sum, ("y", "core"))
            early = stack_up(up + down[:0:-1])
            early_other = swap(early)
            late = turn(above, 1)
        else:
            up.append(turn(up[-1], 1))
            down.append(turn(down[-1], -1))

    delta, plane_sum = after((outer_delta[0], plane_sum))
    pair = (delta.astype(f32) + partner(delta, (1, 0, 3, 2)).astype(f32)).astype(bf16)
    other_pair = partner(pair, (3, 2, 1, 0))

    late_other, blocks = after((swap(late), blocks))
    layer_out, input_grad = project(
        place, tokens, cotangent, early, late, early_other, late_other
    )

    layer_out, other_pair, blocks = after((layer_out, other_pair, blocks))
    summed = pair.astype(f32) + other_pair.astype(f32)
    weight_grad, gain_grad = owner_total(factor, blocks, weight, gain)
    weight_grad = weight_grad.transpose(1, 0, 2)

    chosen = (plan == 1)[:, None, None]
    new_params, new_momentum = outer_step(
        summed / replicas, global_params, momentum, chosen
    )
    return (
        layer_out, input_grad, weight_grad, gain_grad, new_params, new_momentum
    )


def solution(mesh):
    fine = Mesh(mesh.devices.reshape(4, 2, 4, 8, 2), ALL)
    return jax.shard_map(
        local,
        mesh=fine,
        in_specs=(
            P(ALL, None),
            P("rep", FSDP, None),
            P("rep", FSDP),
            P(ALL, None),
            P("rep", None, FSDP, None),
            P(None, FSDP, None),
            P(None, FSDP, None),
            P(),
        ),
        out_specs=(
            P(ALL, None),
            P(ALL, None),
            P("rep", FSDP, None),
            P("rep", FSDP),
            P(None, FSDP, None),
            P(None, FSDP, None),
        ),
        check_vma=False,
    )
```
